32 devices in a mesh: row: 8 (over z, y), col: 4 (over x, core).
Axes of the slice: x: 2, y: 2, z: 4, core: 2. Of those that a mesh axis runs over, the one named last changes fastest.
Arguments:
- features: bfloat16 [4, 1024, 128], P('col', 'row'), may hold values from -6 to 6
- weight: bfloat16 [128, 256], replicated, may hold values from -0.5 to 0.5
- tile_values: bfloat16 [8, 4, 32, 128, 128], P('row', 'col'), may hold values from -0.125 to 0.125
- tile_rows: int32 [8, 4, 32], P('row', 'col'), may hold values from 0 to 3
- tile_cols: int32 [8, 4, 32], P('row', 'col'), may hold values from 0 to 7
- tile_count: int32 [8, 4], P('row', 'col'), may hold values from 4 to 32, as said below
- cotangent: bfloat16 [8, 512, 256], P('row', 'col'), may hold values from -6 to 6
Outputs:
- output: bfloat16 [8, 512, 256], P('row', 'col')
- grad_features: bfloat16 [4, 1024, 128], P('col', 'row')
- weight_grad: float32 [128, 256], replicated
The draws below stay inside these ranges and needn't reach their ends.
Inputs may be any that keep to these rules, and one draw needn't show every extreme that they name: Slots at or beyond a cell's tile_count are ignored; some cell is full in every draw. Tile coordinates within a cell may repeat, and repeated tiles add.
All inputs are finite; a program needn't handle non-finite values.
Results may differ from the reference program's by a relative error of at most 0.022.
Values may be sent and summed in bfloat16 or wider, within the bound.
A program may use at most 64 MiB of HBM per device.

```python
import jax
import jax.numpy as jnp
from jax import lax

F_IN = 128
F_OUT = 256
TB = 128
ROWS_DEV = 128
TILE_CAP = 32
NODES = 4096
TROWS = 4
TCOLS = 8
N_ROW = 8
N_COL = 4


def draw_tile_count(key, part):
    first_key = jax.random.fold_in(key, 11)
    second_key = jax.random.fold_in(key, 23)
    shifts = jax.random.randint(first_key, (N_ROW, N_COL), 0, 4)
    counts = jnp.right_shift(jnp.full((N_ROW, N_COL), TILE_CAP, jnp.int32), shifts.astype(jnp.int32))
    chosen = jax.random.randint(second_key, (), 0, N_ROW * N_COL)
    positions = jnp.arange(N_ROW * N_COL, dtype=jnp.int32).reshape(N_ROW, N_COL)
    return jnp.where(positions == chosen, TILE_CAP, counts).astype(jnp.int32)


def with_ends(result, rng, least, largest):
    longest = result.shape.index(max(result.shape))
    spots = []
    for shift in (0, 1):
        where = [jax.random.randint(jax.random.fold_in(rng, axis), (), 0, length) for axis, length in enumerate(result.shape)]
        where[longest] = (where[longest] + shift) % result.shape[longest]
        spots.append(tuple(where))
    return result.at[spots[0]].set(least).at[spots[1]].set(largest)


def levels(own_key, dims, cuts, least, top_value):
    level, own = 1.0, jax.random.fold_in(own_key, 6)
    for position, parts in cuts:
        draws = jnp.exp(jax.random.uniform(jax.random.fold_in(own, position), (parts,), jnp.float32, least / len(cuts), top_value / len(cuts)))
        level = level * jnp.repeat(draws, dims[position] // parts).reshape([-1 if axis == position else 1 for axis in range(len(dims))])
    return level


def bell_draw(stream_key, extent, deviation, limit, pieces=(), kind=jnp.bfloat16):
    gain = levels(stream_key, extent, pieces, -0.22, 0.18) if pieces else 1.0
    array = jax.random.normal(stream_key, extent, jnp.float32) * deviation * gain
    return jnp.minimum(jnp.maximum(array, -limit), limit).astype(kind)


def setup_inputs(seed: int = 0) -> dict:
    key_of = jax.random.split(jax.random.key(seed), 8)
    features = bell_draw(key_of[0], (N_COL, NODES // N_COL, F_IN), 1.0, 6.0, ((0, 4), (1, 8)))
    weight = bell_draw(key_of[1], (F_IN, F_OUT), F_IN ** -0.5, 0.5)
    tile_values = bell_draw(key_of[2], (N_ROW, N_COL, TILE_CAP, TB, TB), (TILE_CAP * TB * N_COL // (2 * TROWS)) ** -0.5, 0.125, ((0, 8), (1, 4)))
    tile_rows = with_ends(jax.random.randint(key_of[3], (N_ROW, N_COL, TILE_CAP), 0, TROWS), jax.random.fold_in(key_of[3], 1), 0, TROWS - 1).astype(jnp.int32)
    tile_cols = with_ends(jax.random.randint(key_of[4], (N_ROW, N_COL, TILE_CAP), 0, TCOLS), jax.random.fold_in(key_of[4], 1), 0, TCOLS - 1).astype(jnp.int32)
    tile_count = draw_tile_count(jax.random.fold_in(key_of[7], 71), 0)
    cotangent = bell_draw(key_of[6], (N_ROW, NODES // N_ROW, F_OUT), 1.0, 6.0, ((0, 8), (1, 4)))
    return {"features": features, "weight": weight, "tile_values": tile_values, "tile_rows": tile_rows, "tile_cols": tile_cols, "tile_count": tile_count, "cotangent": cotangent}


def spread_tiles(tile_block, target_ids, source_ids, tile_total, source, out_blocks, transpose):
    source_blocks = source[source_ids].astype(jnp.float32)
    block_float = tile_block.astype(jnp.float32)
    if transpose:
        products = jnp.einsum('tij,tif->tjf', block_float, source_blocks, precision=lax.Precision.HIGHEST)
    else:
        products = jnp.einsum('tij,tjf->tif', block_float, source_blocks, precision=lax.Precision.HIGHEST)
    capacity = tile_block.shape[0]
    live_mask = (jnp.arange(capacity, dtype=jnp.int32) < tile_total).astype(jnp.float32)
    products = products * live_mask[:, None, None]
    return jax.ops.segment_sum(products, target_ids, num_segments=out_blocks)


def reference(features, weight, tile_values, tile_rows, tile_cols, tile_count, cotangent):
    col_source = features.reshape(N_COL, TCOLS, TB, F_IN)

    def forward_row(row_pos):
        def add_cell(running, col_pos):
            term = spread_tiles(tile_values[row_pos, col_pos], tile_rows[row_pos, col_pos], tile_cols[row_pos, col_pos], tile_count[row_pos, col_pos], col_source[col_pos], TROWS, False)
            return running + term, None
        running, unused = lax.scan(add_cell, jnp.zeros((TROWS, TB, F_IN), jnp.float32), jnp.arange(N_COL, dtype=jnp.int32))
        return running

    aggregated = lax.map(forward_row, jnp.arange(N_ROW, dtype=jnp.int32)).astype(jnp.bfloat16)
    agg_flat = aggregated.reshape(N_ROW * ROWS_DEV * N_COL, F_IN)
    pre = jnp.dot(agg_flat, weight, preferred_element_type=jnp.float32)
    sigma = jax.nn.sigmoid(pre)
    output = (pre * sigma).astype(jnp.bfloat16).reshape(N_ROW, ROWS_DEV * N_COL, F_OUT)
    slope = sigma * (1.0 + pre * (1.0 - sigma))
    grad_pre = (cotangent.reshape(-1, F_OUT).astype(jnp.float32) * slope).astype(jnp.bfloat16)
    weight_grad = jnp.dot(agg_flat.T, grad_pre, preferred_element_type=jnp.float32) * (NODES ** -0.5)
    grad_agg = jnp.dot(grad_pre, weight.T, preferred_element_type=jnp.float32).astype(jnp.bfloat16)
    row_source = grad_agg.reshape(N_ROW, TROWS, TB, F_IN)

    def backward_col(col_pos):
        def add_cell(running, row_pos):
            term = spread_tiles(tile_values[row_pos, col_pos], tile_cols[row_pos, col_pos], tile_rows[row_pos, col_pos], tile_count[row_pos, col_pos], row_source[row_pos], TCOLS, True)
            return running + term, None
        running, unused = lax.scan(add_cell, jnp.zeros((TCOLS, TB, F_IN), jnp.float32), jnp.arange(N_ROW, dtype=jnp.int32))
        return running

    grad_features = lax.map(backward_col, jnp.arange(N_COL, dtype=jnp.int32))
    grad_features = grad_features.astype(jnp.bfloat16).reshape(N_COL, ROWS_DEV * N_ROW, F_IN)
    return (output, grad_features, weight_grad)
```

```python
import functools

import jax
import jax.numpy as jnp
from jax import lax
from jax.experimental import pallas as pl
from jax.experimental.pallas import tpu as pltpu
from jax.sharding import PartitionSpec as P

MESH = pl.DeviceIdType.MESH
F32 = jnp.float32
BF16 = jnp.bfloat16


def links(cell_rows, cell_cols, tile_rows, tile_cols, tile_total):
    capacity = tile_rows.shape[0]
    slot = jnp.arange(capacity, dtype=jnp.int32)
    key = jnp.where(slot < tile_total, tile_rows * cell_cols + tile_cols, -1)
    blocks = jnp.arange(cell_rows * cell_cols, dtype=jnp.int32)
    wanted = jnp.concatenate([key, blocks])
    limit = jnp.concatenate([slot, jnp.full(blocks.shape, capacity, jnp.int32)])
    hit = (key[None, :] == wanted[:, None]) & (slot[None, :] < limit[:, None])
    found = jnp.max(jnp.where(hit, slot[None, :], -1), axis=1)
    return jnp.where(found < 0, capacity, found)


def kernel(
    R, C, scale,
    link_ref, feat_ref, w_ref, tiles_ref, cot_ref,
    out_ref, gf_ref, wg_ref,
    tiles, cot, sums, dense, fbuf,
    agg_out, agg_in, gbuf, yb_out, yb_in, zb_out, zb_in,
    w1_out, w1_in, w2_out, w2_in, w3, w4,
    local_sem,
    za_s, za_r, ya_s, ya_r, ag_s, ag_r, gb_s, gb_r,
    yb_s, yb_r, zb_s, zb_r, w1_s, w1_r, w2_s, w2_r, w3_s, w3_r, w4_s, w4_r,
):
    row, col = lax.axis_index("row"), lax.axis_index("col")
    H = R // 2
    hi, lo = row // 2, row % 2
    partner = hi * 2 + (1 - lo)
    T = feat_ref.shape[1]
    capacity = tiles.shape[0]
    wrows = w4.shape[1]

    def peer(d):
        return (col + d) % C

    def z_of(k):
        return (hi + k) % H

    def z_from(k):
        return (hi + H - k) % H

    def send(src, dst, s, r, device):
        copy = pltpu.make_async_remote_copy(
            src_ref=src, dst_ref=dst, send_sem=s, recv_sem=r, device_id=device, device_id_type=MESH
        )
        copy.start()
        return copy

    get_tiles = pltpu.make_async_copy(tiles_ref.at[0, 0], tiles, local_sem.at[0])
    get_tiles.start()
    get_cot = pltpu.make_async_copy(cot_ref.at[0], cot, local_sem.at[1])
    get_cot.start()

    barrier = pltpu.get_barrier_semaphore()
    pl.semaphore_signal(barrier, inc=1, device_id=(partner, col), device_id_type=MESH)
    for k in range(1, H):
        pl.semaphore_signal(barrier, inc=1, device_id=(z_of(k) * 2 + lo, col), device_id_type=MESH)
    for d in range(1, C):
        pl.semaphore_signal(barrier, inc=1, device_id=(row, peer(d)), device_id_type=MESH)
    pl.semaphore_wait(barrier, 1 + (H - 1) + (C - 1))

    sent = []
    own_y = send(feat_ref.at[0], fbuf.at[row], ya_s.at[0], ya_r.at[0], (partner, col))
    za = [None]
    for k in range(1, H):
        za.append(send(feat_ref.at[0], fbuf.at[row], za_s.at[k], za_r.at[k], (z_of(k) * 2 + lo, col)))
    fbuf[row] = feat_ref[0]

    sums[capacity] = jnp.zeros(sums.shape[1:], F32)
    get_tiles.wait()

    def add_slot(t, carry):
        sums[t] = tiles[t].astype(F32) + sums[link_ref[t]]
        return carry

    lax.fori_loop(0, capacity, add_slot, 0)

    def place(b, carry):
        i, j = b // R, b % R
        dense[pl.ds(pl.multiple_of(i * T, T), T), pl.ds(pl.multiple_of(j * T, T), T)] = sums[
            link_ref[capacity + b]
        ].astype(BF16)
        return carry

    lax.fori_loop(0, R * C, place, 0)

    ya = [own_y]
    for k in range(1, H):
        za[k].wait_recv()
        block = fbuf.at[z_from(k) * 2 + lo]
        ya.append(send(block, block, ya_s.at[k], ya_r.at[k], (partner, col)))
    for k in range(H):
        ya[k].wait_recv()
    sent += za[1:] + ya

    def aggregate(j):
        rows = dense[pl.ds(pl.multiple_of(j * T, T), T), :]
        return jnp.dot(rows, fbuf[...].reshape(R * T, T), preferred_element_type=F32)

    ag = []
    for d in range(1, C):
        agg_out[d - 1] = aggregate(peer(d)).astype(BF16)
        ag.append(send(agg_out.at[d - 1], agg_in.at[d - 1], ag_s.at[d - 1], ag_r.at[d - 1], (row, peer(d))))
    total = aggregate(col)
    for d in range(1, C):
        ag[d - 1].wait_recv()
        total = total + agg_in[d - 1].astype(F32)
    sent += ag
    agg = total.astype(BF16)

    get_cot.wait()
    pre = jnp.dot(agg, w_ref[...], preferred_element_type=F32)
    sigma = jax.nn.sigmoid(pre)
    slope = sigma * (1.0 + pre * (1.0 - sigma))
    grad_pre = (cot[...].astype(F32) * slope).astype(BF16)
    gbuf[col] = lax.dot_general(
        w_ref[...], grad_pre, (((1,), (1,)), ((), ())), preferred_element_type=F32
    ).astype(BF16)
    gb = []
    for d in range(1, C):
        gb.append(send(gbuf.at[col], gbuf.at[col], gb_s.at[d - 1], gb_r.at[d - 1], (row, peer(d))))
    sent += gb

    agg_t = agg.astype(F32).T.astype(BF16)
    local = jnp.dot(agg_t, grad_pre, preferred_element_type=F32)
    half = local.shape[1] // 2
    local = jnp.concatenate([local[:, :half], local[:, half:]], axis=0)
    for c in range(C):
        w1_out[c] = local[c * wrows : (c + 1) * wrows].astype(BF16)
    w1 = []
    for d in range(1, C):
        w1.append(send(w1_out.at[peer(d)], w1_in.at[d - 1], w1_s.at[d - 1], w1_r.at[d - 1], (row, peer(d))))
    sent += w1
    out_ref[0] = (pre * sigma).astype(BF16)

    for d in range(1, C):
        gb[d - 1].wait_recv()
    source = jnp.concatenate([gbuf[c] for c in range(C)], axis=1)

    def back(i):
        cols = dense[:, pl.ds(pl.multiple_of(i * T, T), T)]
        return jnp.dot(source, cols, preferred_element_type=F32)

    yb = [None] * H
    for k in list(range(1, H)) + [0]:
        yb_out[k] = back(z_of(k) * 2 + (1 - lo)).astype(BF16)
        yb[k] = send(yb_out.at[k], yb_in.at[k], yb_s.at[k], yb_r.at[k], (partner, col))
    sent += yb

    part = w1_out[col].astype(F32)
    for d in range(1, C):
        w1[d - 1].wait_recv()
        part = part + w1_in[d - 1].astype(F32)
    part = part.astype(BF16)
    w2_out[...] = part
    w2 = send(w2_out, w2_in, w2_s.at[0], w2_r.at[0], (partner, col))
    sent.append(w2)

    zb = []
    for k in range(1, H):
        value = back(z_of(k) * 2 + lo)
        yb[k].wait_recv()
        zb_out[k] = (value + yb_in[k].astype(F32)).astype(BF16)
        zb.append(send(zb_out.at[k], zb_in.at[k], zb_s.at[k], zb_r.at[k], (z_of(k) * 2 + lo, col)))
        if k == 1:
            w2.wait_recv()
            w3[hi] = (part.astype(F32) + w2_in[...].astype(F32)).astype(BF16)
            w3_sent = [
                send(w3.at[hi], w3.at[hi], w3_s.at[m], w3_r.at[m], (z_of(m) * 2 + lo, col)) for m in range(1, H)
            ]
    sent += zb + w3_sent
    mine = back(hi * 2 + lo)
    yb[0].wait_recv()
    mine = mine + yb_in[0].astype(F32)

    for copy in w3_sent:
        copy.wait_recv()
    whole = w3[0].astype(F32)
    for h in range(1, H):
        whole = whole + w3[h].astype(F32)
    w4[col] = (whole * scale).astype(BF16)
    w4_sent = [
        send(w4.at[col], w4.at[col], w4_s.at[d - 1], w4_r.at[d - 1], (row, peer(d))) for d in range(1, C)
    ]
    sent += w4_sent

    for k in range(1, H):
        zb[k - 1].wait_recv()
        mine = mine + zb_in[k].astype(F32)
    gf_ref[0] = mine.T.astype(BF16)

    for copy in w4_sent:
        copy.wait_recv()
    full = w4[...].astype(F32).reshape(2, wg_ref.shape[0], half)
    wg_ref[:, :half] = full[0]
    wg_ref[:, half:] = full[1]
    for copy in sent:
        copy.wait_send()


def on_device(features, weight, tile_values, tile_rows, tile_cols, tile_count, cotangent):
    T, width = features.shape[1], features.shape[2]
    hidden = weight.shape[1]
    R, C = lax.axis_size("row"), lax.axis_size("col")
    H = R // 2
    capacity = tile_values.shape[2]
    scale = (T * R * C) ** (-0.5)
    wrows = 2 * width // C
    link = links(C, R, tile_rows[0, 0], tile_cols[0, 0], tile_count[0, 0])
    vmem = pl.BlockSpec(memory_space=pltpu.VMEM)
    smem = pl.BlockSpec(memory_space=pltpu.SMEM)
    hbm = pl.BlockSpec(memory_space=pl.ANY)

    def dma(n):
        return pltpu.SemaphoreType.DMA((n,))

    return pl.pallas_call(
        functools.partial(kernel, R, C, scale),
        out_shape=(
            jax.ShapeDtypeStruct((1, T, hidden), BF16),
            jax.ShapeDtypeStruct((1, T, width), BF16),
            jax.ShapeDtypeStruct((width, hidden), F32),
        ),
        in_specs=[smem, vmem, vmem, hbm, hbm],
        out_specs=(vmem, vmem, vmem),
        scratch_shapes=[
            pltpu.VMEM((capacity, T, T), BF16),
            pltpu.VMEM((T, hidden), BF16),
            pltpu.VMEM((capacity + 1, T, T), F32),
            pltpu.VMEM((C * T, R * T), BF16),
            pltpu.VMEM((R, T, width), BF16),
            pltpu.VMEM((C - 1, T, width), BF16),
            pltpu.VMEM((C - 1, T, width), BF16),
            pltpu.VMEM((C, width, T), BF16),
            pltpu.VMEM((H, width, T), BF16),
            pltpu.VMEM((H, width, T), BF16),
            pltpu.VMEM((H, width, T), BF16),
            pltpu.VMEM((H, width, T), BF16),
            pltpu.VMEM((C, wrows, hidden // 2), BF16),
            pltpu.VMEM((C - 1, wrows, hidden // 2), BF16),
            pltpu.VMEM((wrows, hidden // 2), BF16),
            pltpu.VMEM((wrows, hidden // 2), BF16),
            pltpu.VMEM((H, wrows, hidden // 2), BF16),
            pltpu.VMEM((C, wrows, hidden // 2), BF16),
            dma(2),
            dma(H), dma(H), dma(H), dma(H), dma(C - 1), dma(C - 1), dma(C - 1), dma(C - 1),
            dma(H), dma(H), dma(H), dma(H), dma(C - 1), dma(C - 1), dma(1), dma(1),
            dma(H), dma(H), dma(C - 1), dma(C - 1),
        ],
        compiler_params=pltpu.CompilerParams(
            collective_id=0, has_side_effects=True, vmem_limit_bytes=48 * 1024 * 1024
        ),
    )(link, features, weight, tile_values, cotangent)


def solution(mesh):
    placed = (
        P("col", "row", None),
        P(),
        P("row", "col", None, None, None),
        P("row", "col", None),
        P("row", "col", None),
        P("row", "col"),
        P("row", "col", None),
    )
    return jax.shard_map(
        on_device,
        mesh=mesh,
        in_specs=placed,
        out_specs=(P("row", "col", None), P("col", "row", None), P()),
        check_vma=False,
    )
```

```python
import functools

import jax
import jax.numpy as jnp
from jax import lax
from jax.experimental import pallas as pl
from jax.experimental.pallas import tpu as pltpu
from jax.sharding import PartitionSpec as P

MESH = pl.DeviceIdType.MESH
F32 = jnp.float32
BF16 = jnp.bfloat16


def fill_links(R, C, capacity, rows, cols, total, found):
    width = found.shape[1]
    lane = lax.broadcasted_iota(jnp.int32, (1, width), 1)
    count = total[0, 0]

    def key_of(t):
        return jnp.where(t < count, rows[0, 0, t] * R + cols[0, 0, t], -1)

    keys = jnp.full((1, width), -2, jnp.int32)
    for t in range(capacity):
        keys = jnp.where(lane == t, key_of(t), keys)
    before = jnp.full((1, width), capacity, jnp.int32)
    last = before
    for t in range(capacity):
        key = key_of(t)
        before = jnp.where((keys == key) & (lane > t), t, before)
        last = jnp.where(lane == key, t, last)
    found[0:1, :] = before
    found[1:2, :] = last


def kernel(
    R, C, scale,
    rows_ref, cols_ref, total_ref, feat_ref, weight_ref, tiles_ref, cot_ref,
    out_hbm, gf_hbm, wg_hbm,
    rows, cols, total_s, found, link_ref, w_ref, out_ref, gf_ref, wg_ref,
    tiles, cot, sums, dense, fbuf,
    agg_out, agg_in, gbuf, yb_out, yb_in, zb_out, zb_in,
    w1_out, w1_in, w2_out, w2_in, w3, w4,
    local_sem,
    za_s, za_r, ya_s, ya_r, ag_s, ag_r, gb_s, gb_r,
    yb_s, yb_r, zb_s, zb_r, w1_s, w1_r, w2_s, w2_r, w3_s, w3_r, w4_s, w4_r,
):
    row, col = lax.axis_index("row"), lax.axis_index("col")
    H = R // 2
    hi, lo = row // 2, row % 2
    partner = hi * 2 + (1 - lo)
    T = feat_ref.shape[1]
    capacity = tiles.shape[0]
    wrows = w4.shape[1]

    def peer(d):
        return (col + d) % C

    def z_of(k):
        return (hi + k) % H

    def z_from(k):
        return (hi + H - k) % H

    def send(src, dst, s, r, device):
        copy = pltpu.make_async_remote_copy(
            src_ref=src, dst_ref=dst, send_sem=s, recv_sem=r, device_id=device, device_id_type=MESH
        )
        copy.start()
        return copy

    def fetch(src, dst, n):
        copy = pltpu.make_async_copy(src, dst, local_sem.at[n])
        copy.start()
        return copy

    get_feat = fetch(feat_ref.at[0], fbuf.at[row], 0)
    get_ids = [fetch(rows_ref, rows, 1), fetch(cols_ref, cols, 2), fetch(total_ref, total_s, 3)]
    get_tiles = fetch(tiles_ref.at[0, 0], tiles, 4)
    get_w = fetch(weight_ref, w_ref, 5)
    get_cot = fetch(cot_ref.at[0], cot, 6)

    barrier = pltpu.get_barrier_semaphore()
    pl.semaphore_signal(barrier, inc=1, device_id=(partner, col), device_id_type=MESH)
    for k in range(1, H):
        pl.semaphore_signal(barrier, inc=1, device_id=(z_of(k) * 2 + lo, col), device_id_type=MESH)
    for d in range(1, C):
        pl.semaphore_signal(barrier, inc=1, device_id=(row, peer(d)), device_id_type=MESH)
    sums[capacity] = jnp.zeros(sums.shape[1:], F32)
    for copy in get_ids:
        copy.wait()
    fill_links(R, C, capacity, rows, cols, total_s, found)
    get_links = fetch(found, link_ref, 7)
    get_feat.wait()
    pl.semaphore_wait(barrier, 1 + (H - 1) + (C - 1))

    sent = []
    own_y = send(fbuf.at[row], fbuf.at[row], ya_s.at[0], ya_r.at[0], (partner, col))
    za = [None]
    for k in range(1, H):
        za.append(send(fbuf.at[row], fbuf.at[row], za_s.at[k], za_r.at[k], (z_of(k) * 2 + lo, col)))

    get_tiles.wait()
    get_links.wait()

    def add_slot(t, carry):
        sums[t] = tiles[t].astype(F32) + sums[link_ref[0, t]]
        return carry

    lax.fori_loop(0, capacity, add_slot, 0)

    def place(b, carry):
        i, j = b // R, b % R
        dense[pl.ds(pl.multiple_of(i * T, T), T), pl.ds(pl.multiple_of(j * T, T), T)] = sums[
            link_ref[1, b]
        ].astype(BF16)
        return carry

    lax.fori_loop(0, R * C, place, 0)

    ya = [own_y]
    for k in range(1, H):
        za[k].wait_recv()
        block = fbuf.at[z_from(k) * 2 + lo]
        ya.append(send(block, block, ya_s.at[k], ya_r.at[k], (partner, col)))
    for k in range(H):
        ya[k].wait_recv()
    sent += za[1:] + ya

    def aggregate(j):
        rows = dense[pl.ds(pl.multiple_of(j * T, T), T), :]
        return jnp.dot(rows, fbuf[...].reshape(R * T, T), preferred_element_type=F32)

    ag = []
    for d in range(1, C):
        agg_out[d - 1] = aggregate(peer(d)).astype(BF16)
        ag.append(send(agg_out.at[d - 1], agg_in.at[d - 1], ag_s.at[d - 1], ag_r.at[d - 1], (row, peer(d))))
    total = aggregate(col)
    for d in range(1, C):
        ag[d - 1].wait_recv()
        total = total + agg_in[d - 1].astype(F32)
    sent += ag
    agg = total.astype(BF16)

    get_w.wait()
    get_cot.wait()
    pre = jnp.dot(agg, w_ref[...], preferred_element_type=F32)
    sigma = jax.nn.sigmoid(pre)
    slope = sigma * (1.0 + pre * (1.0 - sigma))
    grad_pre = (cot[...].astype(F32) * slope).astype(BF16)
    gbuf[col] = lax.dot_general(
        w_ref[...], grad_pre, (((1,), (1,)), ((), ())), preferred_element_type=F32
    ).astype(BF16)
    gb = []
    for d in range(1, C):
        gb.append(send(gbuf.at[col], gbuf.at[col], gb_s.at[d - 1], gb_r.at[d - 1], (row, peer(d))))
    sent += gb

    agg_t = agg.astype(F32).T.astype(BF16)
    local = jnp.dot(agg_t, grad_pre, preferred_element_type=F32)
    half = local.shape[1] // 2
    local = jnp.concatenate([local[:, :half], local[:, half:]], axis=0)
    for c in range(C):
        w1_out[c] = local[c * wrows : (c + 1) * wrows].astype(BF16)
    w1 = []
    for d in range(1, C):
        w1.append(send(w1_out.at[peer(d)], w1_in.at[d - 1], w1_s.at[d - 1], w1_r.at[d - 1], (row, peer(d))))
    sent += w1
    out_ref[...] = (pre * sigma).astype(BF16)
    put_out = fetch(out_ref, out_hbm.at[0], 8)

    part = w1_out[col].astype(F32)
    for d in range(1, C):
        w1[d - 1].wait_recv()
        part = part + w1_in[d - 1].astype(F32)
    part = part.astype(BF16)
    w2_out[...] = part
    w2 = send(w2_out, w2_in, w2_s.at[0], w2_r.at[0], (partner, col))
    sent.append(w2)

    for d in range(1, C):
        gb[d - 1].wait_recv()
    source = jnp.concatenate([gbuf[c] for c in range(C)], axis=1)

    def back(i):
        cols = dense[:, pl.ds(pl.multiple_of(i * T, T), T)]
        return jnp.dot(source, cols, preferred_element_type=F32)

    yb = [None] * H
    for k in list(range(1, H)) + [0]:
        yb_out[k] = back(z_of(k) * 2 + (1 - lo)).astype(BF16)
        yb[k] = send(yb_out.at[k], yb_in.at[k], yb_s.at[k], yb_r.at[k], (partner, col))
    sent += yb

    w2.wait_recv()
    w3[hi] = (part.astype(F32) + w2_in[...].astype(F32)).astype(BF16)
    w3_sent = [send(w3.at[hi], w3.at[hi], w3_s.at[m], w3_r.at[m], (z_of(m) * 2 + lo, col)) for m in range(1, H)]
    zb = []
    for k in range(1, H):
        value = back(z_of(k) * 2 + lo)
        yb[k].wait_recv()
        zb_out[k] = (value + yb_in[k].astype(F32)).astype(BF16)
        zb.append(send(zb_out.at[k], zb_in.at[k], zb_s.at[k], zb_r.at[k], (z_of(k) * 2 + lo, col)))
    sent += zb + w3_sent
    mine = back(hi * 2 + lo)
    yb[0].wait_recv()
    mine = mine + yb_in[0].astype(F32)

    for copy in w3_sent:
        copy.wait_recv()
    whole = w3[0].astype(F32)
    for h in range(1, H):
        whole = whole + w3[h].astype(F32)
    w4[col] = (whole * scale).astype(BF16)
    w4_sent = [
        send(w4.at[col], w4.at[col], w4_s.at[d - 1], w4_r.at[d - 1], (row, peer(d))) for d in range(1, C)
    ]
    sent += w4_sent

    for k in range(1, H):
        zb[k - 1].wait_recv()
        mine = mine + zb_in[k].astype(F32)
    gf_ref[...] = mine.T.astype(BF16)
    put_gf = fetch(gf_ref, gf_hbm.at[0], 9)

    for copy in w4_sent:
        copy.wait_recv()
    full = w4[...].astype(F32).reshape(2, wg_ref.shape[0], half)
    wg_ref[:, :half] = full[0]
    wg_ref[:, half:] = full[1]
    put_wg = fetch(wg_ref, wg_hbm, 10)
    for copy in sent:
        copy.wait_send()
    for copy in (put_out, put_gf, put_wg):
        copy.wait()


def hand_on(a, b, c, out_a, out_b, out_c, sem):
    copies = [pltpu.make_async_copy(x, y, sem.at[n]) for n, (x, y) in enumerate([(a, out_a), (b, out_b), (c, out_c)])]
    for copy in copies:
        copy.start()
    for copy in copies:
        copy.wait()


def on_device(features, weight, tile_values, tile_rows, tile_cols, tile_count, cotangent):
    T, width = features.shape[1], features.shape[2]
    hidden = weight.shape[1]
    R, C = lax.axis_size("row"), lax.axis_size("col")
    H = R // 2
    capacity = tile_values.shape[2]
    scale = (T * R * C) ** (-0.5)
    wrows = 2 * width // C
    width_links = -(-max(capacity, R * C) // 128) * 128
    hbm = pl.BlockSpec(memory_space=pltpu.HBM)

    def dma(n):
        return pltpu.SemaphoreType.DMA((n,))

    outs = (
        jax.ShapeDtypeStruct((1, T, hidden), BF16),
        jax.ShapeDtypeStruct((1, T, width), BF16),
        jax.ShapeDtypeStruct((width, hidden), F32),
    )
    results = pl.pallas_call(
        functools.partial(kernel, R, C, scale),
        out_shape=outs,
        in_specs=[hbm] * 7,
        out_specs=(hbm,) * 3,
        scratch_shapes=[
            pltpu.SMEM((1, 1, capacity), jnp.int32),
            pltpu.SMEM((1, 1, capacity), jnp.int32),
            pltpu.SMEM((1, 1), jnp.int32),
            pltpu.VMEM((2, width_links), jnp.int32),
            pltpu.SMEM((2, width_links), jnp.int32),
            pltpu.VMEM((width, hidden), BF16),
            pltpu.VMEM((T, hidden), BF16),
            pltpu.VMEM((T, width), BF16),
            pltpu.VMEM((width, hidden), F32),
            pltpu.VMEM((capacity, T, T), BF16),
            pltpu.VMEM((T, hidden), BF16),
            pltpu.VMEM((capacity + 1, T, T), F32),
            pltpu.VMEM((C * T, R * T), BF16),
            pltpu.VMEM((R, T, width), BF16),
            pltpu.VMEM((C - 1, T, width), BF16),
            pltpu.VMEM((C - 1, T, width), BF16),
            pltpu.VMEM((C, width, T), BF16),
            pltpu.VMEM((H, width, T), BF16),
            pltpu.VMEM((H, width, T), BF16),
            pltpu.VMEM((H, width, T), BF16),
            pltpu.VMEM((H, width, T), BF16),
            pltpu.VMEM((C, wrows, hidden // 2), BF16),
            pltpu.VMEM((C - 1, wrows, hidden // 2), BF16),
            pltpu.VMEM((wrows, hidden // 2), BF16),
            pltpu.VMEM((wrows, hidden // 2), BF16),
            pltpu.VMEM((H, wrows, hidden // 2), BF16),
            pltpu.VMEM((C, wrows, hidden // 2), BF16),
            dma(11),
            dma(H), dma(H), dma(H), dma(H), dma(C - 1), dma(C - 1), dma(C - 1), dma(C - 1),
            dma(H), dma(H), dma(H), dma(H), dma(C - 1), dma(C - 1), dma(1), dma(1),
            dma(H), dma(H), dma(C - 1), dma(C - 1),
        ],
        compiler_params=pltpu.CompilerParams(
            collective_id=0, has_side_effects=True, vmem_limit_bytes=60 * 1024 * 1024
        ),
    )(tile_rows, tile_cols, tile_count, features, weight, tile_values, cotangent)
    return pl.pallas_call(
        hand_on,
        out_shape=outs,
        in_specs=[hbm] * 3,
        out_specs=(hbm,) * 3,
        scratch_shapes=[dma(3)],
        compiler_params=pltpu.CompilerParams(vmem_limit_bytes=60 * 1024 * 1024),
    )(*results)


def solution(mesh):
    placed = (
        P("col", "row", None),
        P(),
        P("row", "col", None, None, None),
        P("row", "col", None),
        P("row", "col", None),
        P("row", "col"),
        P("row", "col", None),
    )
    return jax.shard_map(
        on_device,
        mesh=mesh,
        in_specs=placed,
        out_specs=(P("row", "col", None), P("col", "row", None), P()),
        check_vma=False,
    )
```

```python
import functools

import jax
import jax.numpy as jnp
from jax import lax
from jax.experimental import pallas as pl
from jax.experimental.pallas import tpu as pltpu
from jax.sharding import PartitionSpec as P

MESH = pl.DeviceIdType.MESH
F32 = jnp.float32
BF16 = jnp.bfloat16


def fill_links(R, C, capacity, rows, cols, total, found):
    width = found.shape[1]
    lane = lax.broadcasted_iota(jnp.int32, (1, width), 1)
    count = total[0, 0]

    def key_of(t):
        return jnp.where(t < count, rows[0, 0, t] * R + cols[0, 0, t], -1)

    keys = jnp.full((1, width), -2, jnp.int32)
    for t in range(capacity):
        keys = jnp.where(lane == t, key_of(t), keys)
    before = jnp.full((1, width), capacity, jnp.int32)
    last = before
    for t in range(capacity):
        key = key_of(t)
        before = jnp.where((keys == key) & (lane > t), t, before)
        last = jnp.where(lane == key, t, last)
    found[0:1, :] = before
    found[1:2, :] = last


def kernel(
    R, C, scale,
    rows_ref, cols_ref, total_ref, feat_ref, weight_ref, tiles_ref, cot_ref,
    out_hbm, gf_hbm, wg_hbm,
    rows, cols, total_s, found, link_ref, w_ref, out_ref, gf_ref, wg_ref,
    tiles, cot, sums, dense, fbuf,
    agg_out, agg_in, gbuf, yb_out, yb_in, zb_out, zb_in,
    w1_out, w1_in, w2_out, w2_in, w3, w4,
    local_sem,
    za_s, za_r, ya_s, ya_r, ag_s, ag_r, gb_s, gb_r,
    yb_s, yb_r, zb_s, zb_r, w1_s, w1_r, w2_s, w2_r, w3_s, w3_r, w4_s, w4_r,
):
    row, col = lax.axis_index("row"), lax.axis_index("col")
    H = R // 2
    hi, lo = row // 2, row % 2
    partner = hi * 2 + (1 - lo)
    T = feat_ref.shape[1]
    capacity = tiles.shape[0]
    wrows = w4.shape[1]

    def peer(d):
        return (col + d) % C

    def z_of(k):
        other, bit = hi, 1
        while bit < H:
            if k & bit:
                other = other + bit * (1 - 2 * ((hi // bit) % 2))
            bit *= 2
        return other

    def send(src, dst, s, r, device):
        copy = pltpu.make_async_remote_copy(
            src_ref=src, dst_ref=dst, send_sem=s, recv_sem=r, device_id=device, device_id_type=MESH
        )
        copy.start()
        return copy

    def fetch(src, dst, n):
        copy = pltpu.make_async_copy(src, dst, local_sem.at[n])
        copy.start()
        return copy

    get_feat = fetch(feat_ref.at[0], fbuf.at[row], 0)
    get_ids = [fetch(rows_ref, rows, 1), fetch(cols_ref, cols, 2), fetch(total_ref, total_s, 3)]
    get_tiles = fetch(tiles_ref.at[0, 0], tiles, 4)
    get_w = fetch(weight_ref, w_ref, 5)
    get_cot = fetch(cot_ref.at[0], cot, 6)

    barrier = pltpu.get_barrier_semaphore()
    pl.semaphore_signal(barrier, inc=1, device_id=(partner, col), device_id_type=MESH)
    for k in range(1, H):
        pl.semaphore_signal(barrier, inc=1, device_id=(z_of(k) * 2 + lo, col), device_id_type=MESH)
    for d in range(1, C):
        pl.semaphore_signal(barrier, inc=1, device_id=(row, peer(d)), device_id_type=MESH)
    get_feat.wait()
    pl.semaphore_wait(barrier, 1 + (H - 1) + (C - 1))

    sent = []
    own_y = send(fbuf.at[row], fbuf.at[row], ya_s.at[0], ya_r.at[0], (partner, col))
    za = [None]
    for k in range(1, H):
        za.append(send(fbuf.at[row], fbuf.at[row], za_s.at[k], za_r.at[k], (z_of(k) * 2 + lo, col)))

    sums[capacity] = jnp.zeros(sums.shape[1:], F32)
    for copy in get_ids:
        copy.wait()
    fill_links(R, C, capacity, rows, cols, total_s, found)
    get_links = fetch(found, link_ref, 7)
    get_tiles.wait()
    get_links.wait()

    def add_slot(t, carry):
        sums[t] = tiles[t].astype(F32) + sums[link_ref[0, t]]
        return carry

    lax.fori_loop(0, capacity, add_slot, 0, unroll=2)

    ya = [own_y]

    def forward(k):
        za[k].wait_recv()
        block = fbuf.at[z_of(k) * 2 + lo]
        ya.append(send(block, block, ya_s.at[k], ya_r.at[k], (partner, col)))

    forward(1)

    def place(b, carry):
        i, j = b // R, b % R
        dense[pl.ds(pl.multiple_of(i * T, T), T), pl.ds(pl.multiple_of(j * T, T), T)] = sums[
            link_ref[1, b]
        ].astype(BF16)
        return carry

    lax.fori_loop(0, R * C, place, 0, unroll=4)

    for k in range(2, H):
        forward(k)
    for k in range(H):
        ya[k].wait_recv()
    sent += za[1:] + ya

    def aggregate(j):
        rows = dense[pl.ds(pl.multiple_of(j * T, T), T), :]
        return jnp.dot(rows, fbuf[...].reshape(R * T, T), preferred_element_type=F32)

    ag = []
    for d in range(1, C):
        agg_out[d - 1] = aggregate(peer(d)).astype(BF16)
        ag.append(send(agg_out.at[d - 1], agg_in.at[d - 1], ag_s.at[d - 1], ag_r.at[d - 1], (row, peer(d))))
    total = aggregate(col)
    for d in range(1, C):
        ag[d - 1].wait_recv()
        total = total + agg_in[d - 1].astype(F32)
    sent += ag
    agg = total.astype(BF16)

    get_w.wait()
    get_cot.wait()
    pre = jnp.dot(agg, w_ref[...], preferred_element_type=F32)
    sigma = jax.nn.sigmoid(pre)
    slope = sigma * (1.0 + pre * (1.0 - sigma))
    grad_pre = (cot[...].astype(F32) * slope).astype(BF16)
    gbuf[col] = lax.dot_general(
        w_ref[...], grad_pre, (((1,), (1,)), ((), ())), preferred_element_type=F32
    ).astype(BF16)
    gb = []
    for d in range(1, C):
        gb.append(send(gbuf.at[col], gbuf.at[col], gb_s.at[d - 1], gb_r.at[d - 1], (row, peer(d))))
    sent += gb

    agg_t = agg.astype(F32).T.astype(BF16)
    local = jnp.dot(agg_t, grad_pre, preferred_element_type=F32)
    half = local.shape[1] // 2
    local = jnp.concatenate([local[:, :half], local[:, half:]], axis=0)
    for c in range(C):
        w1_out[c] = local[c * wrows : (c + 1) * wrows].astype(BF16)
    w1 = []
    for d in range(1, C):
        w1.append(send(w1_out.at[peer(d)], w1_in.at[d - 1], w1_s.at[d - 1], w1_r.at[d - 1], (row, peer(d))))
    sent += w1
    out_ref[...] = (pre * sigma).astype(BF16)
    put_out = fetch(out_ref, out_hbm.at[0], 8)

    part = w1_out[col].astype(F32)
    for d in range(1, C):
        w1[d - 1].wait_recv()
        part = part + w1_in[d - 1].astype(F32)
    part = part.astype(BF16)
    w2_out[...] = part
    w2 = send(w2_out, w2_in, w2_s.at[0], w2_r.at[0], (partner, col))
    sent.append(w2)

    for d in range(1, C):
        gb[d - 1].wait_recv()
    source = jnp.concatenate([gbuf[c] for c in range(C)], axis=1)

    def back(i):
        cols = dense[:, pl.ds(pl.multiple_of(i * T, T), T)]
        return jnp.dot(source, cols, preferred_element_type=F32)

    yb = [None] * H
    far = list(range(2, H)) + [1]
    for k in far + [0]:
        yb_out[k] = back(z_of(k) * 2 + (1 - lo)).astype(BF16)
        yb[k] = send(yb_out.at[k], yb_in.at[k], yb_s.at[k], yb_r.at[k], (partner, col))
    sent += yb

    w2.wait_recv()
    w3[hi] = (part.astype(F32) + w2_in[...].astype(F32)).astype(BF16)
    w3_sent = [send(w3.at[hi], w3.at[hi], w3_s.at[m], w3_r.at[m], (z_of(m) * 2 + lo, col)) for m in range(1, H)]
    zb = []
    for k in far:
        value = back(z_of(k) * 2 + lo)
        yb[k].wait_recv()
        zb_out[k] = (value + yb_in[k].astype(F32)).astype(BF16)
        zb.append(send(zb_out.at[k], zb_in.at[k], zb_s.at[k], zb_r.at[k], (z_of(k) * 2 + lo, col)))
    sent += zb + w3_sent
    mine = back(hi * 2 + lo)
    yb[0].wait_recv()
    mine = mine + yb_in[0].astype(F32)

    for copy in w3_sent:
        copy.wait_recv()
    whole = w3[0].astype(F32)
    for h in range(1, H):
        whole = whole + w3[h].astype(F32)
    w4[col] = (whole * scale).astype(BF16)
    w4_sent = [
        send(w4.at[col], w4.at[col], w4_s.at[d - 1], w4_r.at[d - 1], (row, peer(d))) for d in range(1, C)
    ]
    sent += w4_sent

    for copy in zb:
        copy.wait_recv()
    for k in range(1, H):
        mine = mine + zb_in[k].astype(F32)
    gf_ref[...] = mine.T.astype(BF16)
    put_gf = fetch(gf_ref, gf_hbm.at[0], 9)

    for copy in w4_sent:
        copy.wait_recv()
    full = w4[...].astype(F32).reshape(2, wg_ref.shape[0], half)
    wg_ref[:, :half] = full[0]
    wg_ref[:, half:] = full[1]
    put_wg = fetch(wg_ref, wg_hbm, 10)
    for copy in sent:
        copy.wait_send()
    for copy in (put_out, put_gf, put_wg):
        copy.wait()


def on_device(features, weight, tile_values, tile_rows, tile_cols, tile_count, cotangent):
    T, width = features.shape[1], features.shape[2]
    hidden = weight.shape[1]
    R, C = lax.axis_size("row"), lax.axis_size("col")
    H = R // 2
    capacity = tile_values.shape[2]
    scale = (T * R * C) ** (-0.5)
    wrows = 2 * width // C
    width_links = -(-max(capacity, R * C) // 128) * 128
    hbm = pl.BlockSpec(memory_space=pltpu.HBM)

    def dma(n):
        return pltpu.SemaphoreType.DMA((n,))

    outs = (
        jax.ShapeDtypeStruct((1, T, hidden), BF16),
        jax.ShapeDtypeStruct((1, T, width), BF16),
        jax.ShapeDtypeStruct((width, hidden), F32),
    )
    return pl.pallas_call(
        functools.partial(kernel, R, C, scale),
        out_shape=outs,
        in_specs=[hbm] * 7,
        out_specs=(hbm,) * 3,
        scratch_shapes=[
            pltpu.SMEM((1, 1, capacity), jnp.int32),
            pltpu.SMEM((1, 1, capacity), jnp.int32),
            pltpu.SMEM((1, 1), jnp.int32),
            pltpu.VMEM((2, width_links), jnp.int32),
            pltpu.SMEM((2, width_links), jnp.int32),
            pltpu.VMEM((width, hidden), BF16),
            pltpu.VMEM((T, hidden), BF16),
            pltpu.VMEM((T, width), BF16),
            pltpu.VMEM((width, hidden), F32),
            pltpu.VMEM((capacity, T, T), BF16),
            pltpu.VMEM((T, hidden), BF16),
            pltpu.VMEM((capacity + 1, T, T), F32),
            pltpu.VMEM((C * T, R * T), BF16),
            pltpu.VMEM((R, T, width), BF16),
            pltpu.VMEM((C - 1, T, width), BF16),
            pltpu.VMEM((C - 1, T, width), BF16),
            pltpu.VMEM((C, width, T), BF16),
            pltpu.VMEM((H, width, T), BF16),
            pltpu.VMEM((H, width, T), BF16),
            pltpu.VMEM((H, width, T), BF16),
            pltpu.VMEM((H, width, T), BF16),
            pltpu.VMEM((C, wrows, hidden // 2), BF16),
            pltpu.VMEM((C - 1, wrows, hidden // 2), BF16),
            pltpu.VMEM((wrows, hidden // 2), BF16),
            pltpu.VMEM((wrows, hidden // 2), BF16),
            pltpu.VMEM((H, wrows, hidden // 2), BF16),
            pltpu.VMEM((C, wrows, hidden // 2), BF16),
            dma(11),
            dma(H), dma(H), dma(H), dma(H), dma(C - 1), dma(C - 1), dma(C - 1), dma(C - 1),
            dma(H), dma(H), dma(H), dma(H), dma(C - 1), dma(C - 1), dma(1), dma(1),
            dma(H), dma(H), dma(C - 1), dma(C - 1),
        ],
        compiler_params=pltpu.CompilerParams(
            collective_id=0, has_side_effects=True, vmem_limit_bytes=60 * 1024 * 1024
        ),
    )(tile_rows, tile_cols, tile_count, features, weight, tile_values, cotangent)


def solution(mesh):
    placed = (
        P("col", "row", None),
        P(),
        P("row", "col", None, None, None),
        P("row", "col", None),
        P("row", "col", None),
        P("row", "col"),
        P("row", "col", None),
    )
    return jax.shard_map(
        on_device,
        mesh=mesh,
        in_specs=placed,
        out_specs=(P("row", "col", None), P("col", "row", None), P()),
        check_vma=False,
    )
```

```python
import functools

import jax
import jax.numpy as jnp
from jax import lax
from jax.experimental import pallas as pl
from jax.experimental.pallas import tpu as pltpu
from jax.sharding import PartitionSpec as P

MESH = pl.DeviceIdType.MESH
F32 = jnp.float32
BF16 = jnp.bfloat16


def fill_links(R, C, capacity, rows, cols, total, found):
    width = found.shape[1]
    lane = lax.broadcasted_iota(jnp.int32, (1, width), 1)
    count = total[0, 0]

    def key_of(t):
        return jnp.where(t < count, rows[0, 0, t] * R + cols[0, 0, t], -1)

    keys = jnp.full((1, width), -2, jnp.int32)
    for t in range(capacity):
        keys = jnp.where(lane == t, key_of(t), keys)
    before = jnp.full((1, width), capacity, jnp.int32)
    last = before
    for t in range(capacity):
        key = key_of(t)
        before = jnp.where((keys == key) & (lane > t), t, before)
        last = jnp.where(lane == key, t, last)
    found[0:1, :] = before
    found[1:2, :] = last


def kernel(
    R, C, scale,
    rows_ref, cols_ref, total_ref, feat_ref, weight_ref, tiles_ref, cot_ref,
    out_hbm, gf_hbm, wg_hbm,
    rows, cols, total_s, found, link_ref, w_ref, out_ref, gf_ref, wg_ref,
    tiles, cot, sums, dense, fbuf,
    agg_out, agg_in, gbuf, yb_out, yb_in, zb_out, zb_in,
    w1_out, w1_in, w2_out, w2_in, w3, w4,
    local_sem,
    za_s, za_r, ya_s, ya_r, ag_s, ag_r, gb_s, gb_r,
    yb_s, yb_r, zb_s, zb_r, w1_s, w1_r, w2_s, w2_r, w3_s, w3_r, w4_s, w4_r,
):
    row, col = lax.axis_index("row"), lax.axis_index("col")
    H = R // 2
    hi, lo = row // 2, row % 2
    partner = hi * 2 + (1 - lo)
    T = feat_ref.shape[1]
    capacity = tiles.shape[0]
    wrows = w4.shape[1]

    def peer(d):
        return (col + d) % C

    def z_of(k):
        other, bit = hi, 1
        while bit < H:
            if k & bit:
                other = other + bit * (1 - 2 * ((hi // bit) % 2))
            bit *= 2
        return other

    def send(src, dst, s, r, device):
        copy = pltpu.make_async_remote_copy(
            src_ref=src, dst_ref=dst, send_sem=s, recv_sem=r, device_id=device, device_id_type=MESH
        )
        copy.start()
        return copy

    def fetch(src, dst, n):
        copy = pltpu.make_async_copy(src, dst, local_sem.at[n])
        copy.start()
        return copy

    get_feat = fetch(feat_ref.at[0], fbuf.at[row], 0)
    get_ids = [fetch(rows_ref, rows, 1), fetch(cols_ref, cols, 2), fetch(total_ref, total_s, 3)]
    get_tiles = fetch(tiles_ref.at[0, 0], tiles, 4)
    get_w = fetch(weight_ref, w_ref, 5)
    get_cot = fetch(cot_ref.at[0], cot, 6)

    barrier = pltpu.get_barrier_semaphore()
    pl.semaphore_signal(barrier, inc=1, device_id=(partner, col), device_id_type=MESH)
    for k in range(1, H):
        pl.semaphore_signal(barrier, inc=1, device_id=(z_of(k) * 2 + lo, col), device_id_type=MESH)
    for d in range(1, C):
        pl.semaphore_signal(barrier, inc=1, device_id=(row, peer(d)), device_id_type=MESH)
    get_feat.wait()
    pl.semaphore_wait(barrier, 1 + (H - 1) + (C - 1))

    sent = []
    own_y = send(fbuf.at[row], fbuf.at[row], ya_s.at[0], ya_r.at[0], (partner, col))
    za = [None]
    for k in range(1, H):
        za.append(send(fbuf.at[row], fbuf.at[row], za_s.at[k], za_r.at[k], (z_of(k) * 2 + lo, col)))

    sums[capacity] = jnp.zeros(sums.shape[1:], F32)
    for copy in get_ids:
        copy.wait()
    fill_links(R, C, capacity, rows, cols, total_s, found)
    get_links = fetch(found, link_ref, 7)
    ya = [own_y]

    def forward(k):
        za[k].wait_recv()
        block = fbuf.at[z_of(k) * 2 + lo]
        ya.append(send(block, block, ya_s.at[k], ya_r.at[k], (partner, col)))

    forward(1)
    get_tiles.wait()
    get_links.wait()

    def add_slot(t, carry):
        sums[t] = tiles[t].astype(F32) + sums[link_ref[0, t]]
        return carry

    lax.fori_loop(0, capacity, add_slot, 0, unroll=2)

    for k in range(2, min(3, H)):
        forward(k)

    def place(b, carry):
        i, j = b // R, b % R
        dense[pl.ds(pl.multiple_of(i * T, T), T), pl.ds(pl.multiple_of(j * T, T), T)] = sums[
            link_ref[1, b]
        ].astype(BF16)
        return carry

    lax.fori_loop(0, R * C, place, 0, unroll=4)

    for k in range(3, H):
        forward(k)
    for k in range(H):
        ya[k].wait_recv()
    sent += za[1:] + ya

    def aggregate(j):
        rows = dense[pl.ds(pl.multiple_of(j * T, T), T), :]
        return jnp.dot(rows, fbuf[...].reshape(R * T, T), preferred_element_type=F32)

    ag = []
    for d in range(1, C):
        agg_out[d - 1] = aggregate(peer(d)).astype(BF16)
        ag.append(send(agg_out.at[d - 1], agg_in.at[d - 1], ag_s.at[d - 1], ag_r.at[d - 1], (row, peer(d))))
    total = aggregate(col)
    for d in range(1, C):
        ag[d - 1].wait_recv()
        total = total + agg_in[d - 1].astype(F32)
    sent += ag
    agg = total.astype(BF16)

    get_w.wait()
    get_cot.wait()
    pre = jnp.dot(agg, w_ref[...], preferred_element_type=F32)
    sigma = jax.nn.sigmoid(pre)
    slope = sigma * (1.0 + pre * (1.0 - sigma))
    grad_pre = (cot[...].astype(F32) * slope).astype(BF16)
    gbuf[col] = lax.dot_general(
        w_ref[...], grad_pre, (((1,), (1,)), ((), ())), preferred_element_type=F32
    ).astype(BF16)
    gb = []
    for d in range(1, C):
        gb.append(send(gbuf.at[col], gbuf.at[col], gb_s.at[d - 1], gb_r.at[d - 1], (row, peer(d))))
    sent += gb

    agg_t = agg.astype(F32).T.astype(BF16)
    local = jnp.dot(agg_t, grad_pre, preferred_element_type=F32)
    half = local.shape[1] // 2
    local = jnp.concatenate([local[:, :half], local[:, half:]], axis=0)
    for c in range(C):
        w1_out[c] = local[c * wrows : (c + 1) * wrows].astype(BF16)
    w1 = []
    for d in range(1, C):
        w1.append(send(w1_out.at[peer(d)], w1_in.at[d - 1], w1_s.at[d - 1], w1_r.at[d - 1], (row, peer(d))))
    sent += w1
    out_ref[0] = (pre * sigma).astype(BF16)
    put_out = fetch(out_ref, out_hbm, 8)

    for d in range(1, C):
        gb[d - 1].wait_recv()
    source = jnp.concatenate([gbuf[c] for c in range(C)], axis=1)

    def back(i):
        cols = dense[:, pl.ds(pl.multiple_of(i * T, T), T)]
        return jnp.dot(source, cols, preferred_element_type=F32)

    yb = [None] * H
    far = list(range(2, H)) + [1]

    def back_y(k):
        yb_out[k] = back(z_of(k) * 2 + (1 - lo)).astype(BF16)
        yb[k] = send(yb_out.at[k], yb_in.at[k], yb_s.at[k], yb_r.at[k], (partner, col))

    for k in far[:2]:
        back_y(k)
    part = w1_out[col].astype(F32)
    for d in range(1, C):
        w1[d - 1].wait_recv()
        part = part + w1_in[d - 1].astype(F32)
    part = part.astype(BF16)
    w2_out[...] = part
    w2 = send(w2_out, w2_in, w2_s.at[0], w2_r.at[0], (partner, col))
    sent.append(w2)

    for k in far[2:] + [0]:
        back_y(k)
    sent += yb

    zb = []

    def back_z(k):
        value = back(z_of(k) * 2 + lo)
        yb[k].wait_recv()
        zb_out[k] = (value + yb_in[k].astype(F32)).astype(BF16)
        zb.append(send(zb_out.at[k], zb_in.at[k], zb_s.at[k], zb_r.at[k], (z_of(k) * 2 + lo, col)))

    back_z(far[0])
    w2.wait_recv()
    w3[hi] = (part.astype(F32) + w2_in[...].astype(F32)).astype(BF16)
    w3_sent = [send(w3.at[hi], w3.at[hi], w3_s.at[m], w3_r.at[m], (z_of(m) * 2 + lo, col)) for m in range(1, H)]
    for k in far[1:]:
        back_z(k)
    sent += zb + w3_sent
    mine = back(hi * 2 + lo)
    yb[0].wait_recv()
    mine = mine + yb_in[0].astype(F32)

    for copy in w3_sent:
        copy.wait_recv()
    whole = w3[0].astype(F32)
    for h in range(1, H):
        whole = whole + w3[h].astype(F32)
    w4[col] = (whole * scale).astype(BF16)
    w4_sent = [
        send(w4.at[col], w4.at[col], w4_s.at[d - 1], w4_r.at[d - 1], (row, peer(d))) for d in range(1, C)
    ]
    sent += w4_sent

    for copy in zb:
        copy.wait_recv()
    for k in range(1, H):
        mine = mine + zb_in[k].astype(F32)
    gf_ref[0] = mine.T.astype(BF16)
    put_gf = fetch(gf_ref, gf_hbm, 9)

    for copy in w4_sent:
        copy.wait_recv()
    full = w4[...].astype(F32).reshape(2, wg_ref.shape[0], half)
    wg_ref[:, :half] = full[0]
    wg_ref[:, half:] = full[1]
    put_wg = fetch(wg_ref, wg_hbm, 10)
    for copy in sent:
        copy.wait_send()
    for copy in (put_out, put_gf, put_wg):
        copy.wait()


def hand_on(*refs):
    sources, targets, held, sem = refs[:3], refs[3:6], refs[6:9], refs[9]
    reads = [pltpu.make_async_copy(sources[n], held[n], sem.at[n]) for n in range(3)]
    writes = [pltpu.make_async_copy(held[n], targets[n], sem.at[3 + n]) for n in range(3)]
    for copy in reads:
        copy.start()
    for read, write in zip(reads, writes):
        read.wait()
        write.start()
    for copy in writes:
        copy.wait()


def on_device(features, weight, tile_values, tile_rows, tile_cols, tile_count, cotangent):
    T, width = features.shape[1], features.shape[2]
    hidden = weight.shape[1]
    R, C = lax.axis_size("row"), lax.axis_size("col")
    H = R // 2
    capacity = tile_values.shape[2]
    scale = (T * R * C) ** (-0.5)
    wrows = 2 * width // C
    width_links = -(-max(capacity, R * C) // 128) * 128
    hbm = pl.BlockSpec(memory_space=pltpu.HBM)

    def dma(n):
        return pltpu.SemaphoreType.DMA((n,))

    outs = (
        jax.ShapeDtypeStruct((1, T, hidden), BF16),
        jax.ShapeDtypeStruct((1, T, width), BF16),
        jax.ShapeDtypeStruct((width, hidden), F32),
    )
    results = pl.pallas_call(
        functools.partial(kernel, R, C, scale),
        out_shape=outs,
        in_specs=[hbm] * 7,
        out_specs=(hbm,) * 3,
        scratch_shapes=[
            pltpu.SMEM((1, 1, capacity), jnp.int32),
            pltpu.SMEM((1, 1, capacity), jnp.int32),
            pltpu.SMEM((1, 1), jnp.int32),
            pltpu.VMEM((2, width_links), jnp.int32),
            pltpu.SMEM((2, width_links), jnp.int32),
            pltpu.VMEM((width, hidden), BF16),
            *[pltpu.VMEM(o.shape, o.dtype) for o in outs],
            pltpu.VMEM((capacity, T, T), BF16),
            pltpu.VMEM((T, hidden), BF16),
            pltpu.VMEM((capacity + 1, T, T), F32),
            pltpu.VMEM((C * T, R * T), BF16),
            pltpu.VMEM((R, T, width), BF16),
            pltpu.VMEM((C - 1, T, width), BF16),
            pltpu.VMEM((C - 1, T, width), BF16),
            pltpu.VMEM((C, width, T), BF16),
            pltpu.VMEM((H, width, T), BF16),
            pltpu.VMEM((H, width, T), BF16),
            pltpu.VMEM((H, width, T), BF16),
            pltpu.VMEM((H, width, T), BF16),
            pltpu.VMEM((C, wrows, hidden // 2), BF16),
            pltpu.VMEM((C - 1, wrows, hidden // 2), BF16),
            pltpu.VMEM((wrows, hidden // 2), BF16),
            pltpu.VMEM((wrows, hidden // 2), BF16),
            pltpu.VMEM((H, wrows, hidden // 2), BF16),
            pltpu.VMEM((C, wrows, hidden // 2), BF16),
            dma(11),
            dma(H), dma(H), dma(H), dma(H), dma(C - 1), dma(C - 1), dma(C - 1), dma(C - 1),
            dma(H), dma(H), dma(H), dma(H), dma(C - 1), dma(C - 1), dma(1), dma(1),
            dma(H), dma(H), dma(C - 1), dma(C - 1),
        ],
        compiler_params=pltpu.CompilerParams(
            collective_id=0, has_side_effects=True, vmem_limit_bytes=60 * 1024 * 1024
        ),
    )(tile_rows, tile_cols, tile_count, features, weight, tile_values, cotangent)
    return pl.pallas_call(
        hand_on,
        out_shape=outs,
        in_specs=[hbm] * 3,
        out_specs=(hbm,) * 3,
        scratch_shapes=[*[pltpu.VMEM(o.shape, o.dtype) for o in outs], dma(6)],
        compiler_params=pltpu.CompilerParams(vmem_limit_bytes=60 * 1024 * 1024),
    )(*results)


def solution(mesh):
    placed = (
        P("col", "row", None),
        P(),
        P("row", "col", None, None, None),
        P("row", "col", None),
        P("row", "col", None),
        P("row", "col"),
        P("row", "col", None),
    )
    return jax.shard_map(
        on_device,
        mesh=mesh,
        in_specs=placed,
        out_specs=(P("row", "col", None), P("col", "row", None), P()),
        check_vma=False,
    )
```

```python
import functools

import jax
import jax.numpy as jnp
from jax import lax
from jax.experimental import pallas as pl
from jax.experimental.pallas import tpu as pltpu
from jax.sharding import PartitionSpec as P

MESH = pl.DeviceIdType.MESH
F32 = jnp.float32
BF16 = jnp.bfloat16


def fill_links(R, C, capacity, rows, cols, total, found):
    width = found.shape[1]
    lane = lax.broadcasted_iota(jnp.int32, (1, width), 1)
    count = total[0, 0]

    def key_of(t):
        return jnp.where(t < count, rows[0, 0, t] * R + cols[0, 0, t], -1)

    keys = jnp.full((1, width), -2, jnp.int32)
    for t in range(capacity):
        keys = jnp.where(lane == t, key_of(t), keys)
    before = jnp.full((1, width), capacity, jnp.int32)
    last = before
    for t in range(capacity):
        key = key_of(t)
        before = jnp.where((keys == key) & (lane > t), t, before)
        last = jnp.where(lane == key, t, last)
    found[0:1, :] = before
    found[1:2, :] = last


def kernel(
    R, C, scale,
    rows_ref, cols_ref, total_ref, feat_ref, weight_ref, tiles_ref, cot_ref,
    out_hbm, gf_hbm, wg_hbm,
    rows, cols, total_s, found, link_ref, w_ref, out_ref, gf_ref, wg_ref,
    tiles, cot, sums, dense, fbuf,
    agg_out, agg_in, gbuf, yb_out, yb_in, zb_out, zb_in,
    w1_out, w1_in, w3, w4,
    local_sem,
    za_s, za_r, ya_s, ya_r, ag_s, ag_r, gb_s, gb_r,
    yb_s, yb_r, zb_s, zb_r, w1_s, w1_r, w3_s, w3_r, w4_s, w4_r,
):
    row, col = lax.axis_index("row"), lax.axis_index("col")
    H = R // 2
    hi, lo = row // 2, row % 2
    partner = hi * 2 + (1 - lo)
    T = feat_ref.shape[1]
    capacity = tiles.shape[0]
    wrows = w4.shape[1]

    def peer(d):
        return (col + d) % C

    def z_of(k):
        other, bit = hi, 1
        while bit < H:
            if k & bit:
                other = other + bit * (1 - 2 * ((hi // bit) % 2))
            bit *= 2
        return other

    def send(src, dst, s, r, device):
        copy = pltpu.make_async_remote_copy(
            src_ref=src, dst_ref=dst, send_sem=s, recv_sem=r, device_id=device, device_id_type=MESH
        )
        copy.start()
        return copy

    def fetch(src, dst, n):
        copy = pltpu.make_async_copy(src, dst, local_sem.at[n])
        copy.start()
        return copy

    get_feat = fetch(feat_ref.at[0], fbuf.at[row], 0)
    get_ids = [fetch(rows_ref, rows, 1), fetch(cols_ref, cols, 2), fetch(total_ref, total_s, 3)]
    get_tiles = fetch(tiles_ref.at[0, 0], tiles, 4)
    get_w = fetch(weight_ref, w_ref, 5)
    get_cot = fetch(cot_ref.at[0], cot, 6)

    barrier = pltpu.get_barrier_semaphore()
    for n in range(1, R):
        pl.semaphore_signal(barrier, inc=1, device_id=((row + n) % R, col), device_id_type=MESH)
    for d in range(1, C):
        pl.semaphore_signal(barrier, inc=1, device_id=(row, peer(d)), device_id_type=MESH)
    get_feat.wait()
    pl.semaphore_wait(barrier, (R - 1) + (C - 1))

    sent = []
    own_y = send(fbuf.at[row], fbuf.at[row], ya_s.at[0], ya_r.at[0], (partner, col))
    za = [None]
    for k in range(1, H):
        za.append(send(fbuf.at[row], fbuf.at[row], za_s.at[k], za_r.at[k], (z_of(k) * 2 + lo, col)))

    sums[capacity] = jnp.zeros(sums.shape[1:], F32)
    for copy in get_ids:
        copy.wait()
    fill_links(R, C, capacity, rows, cols, total_s, found)
    get_links = fetch(found, link_ref, 7)
    ya = [own_y]

    def forward(k):
        za[k].wait_recv()
        block = fbuf.at[z_of(k) * 2 + lo]
        ya.append(send(block, block, ya_s.at[k], ya_r.at[k], (partner, col)))

    get_tiles.wait()
    get_links.wait()

    def add_slot(t, carry):
        sums[t] = tiles[t].astype(F32) + sums[link_ref[0, t]]
        return carry

    lax.fori_loop(0, capacity, add_slot, 0, unroll=2)

    forward(1)

    def place(b, carry):
        i, j = b // R, b % R
        dense[pl.ds(pl.multiple_of(i * T, T), T), pl.ds(pl.multiple_of(j * T, T), T)] = sums[
            link_ref[1, b]
        ].astype(BF16)
        return carry

    lax.fori_loop(0, R * C, place, 0, unroll=4)

    for k in range(2, H):
        forward(k)
    for k in range(H):
        ya[k].wait_recv()
    sent += za[1:] + ya

    def aggregate(j):
        rows = dense[pl.ds(pl.multiple_of(j * T, T), T), :]
        return jnp.dot(rows, fbuf[...].reshape(R * T, T), preferred_element_type=F32)

    ag = []
    for d in range(1, C):
        agg_out[d - 1] = aggregate(peer(d)).astype(BF16)
        ag.append(send(agg_out.at[d - 1], agg_in.at[d - 1], ag_s.at[d - 1], ag_r.at[d - 1], (row, peer(d))))
    total = aggregate(col)
    for d in range(1, C):
        ag[d - 1].wait_recv()
        total = total + agg_in[d - 1].astype(F32)
    sent += ag
    agg = total.astype(BF16)

    get_w.wait()
    get_cot.wait()
    pre = jnp.dot(agg, w_ref[...], preferred_element_type=F32)
    sigma = jax.nn.sigmoid(pre)
    slope = sigma * (1.0 + pre * (1.0 - sigma))
    grad_pre = (cot[...].astype(F32) * slope).astype(BF16)
    gbuf[col] = lax.dot_general(
        w_ref[...], grad_pre, (((1,), (1,)), ((), ())), preferred_element_type=F32
    ).astype(BF16)
    gb = []
    for d in range(1, C):
        gb.append(send(gbuf.at[col], gbuf.at[col], gb_s.at[d - 1], gb_r.at[d - 1], (row, peer(d))))
    sent += gb

    agg_t = agg.astype(F32).T.astype(BF16)
    local = jnp.dot(agg_t, grad_pre, preferred_element_type=F32)
    half = local.shape[1] // 2
    local = jnp.concatenate([local[:, :half], local[:, half:]], axis=0)
    for c in range(C):
        w1_out[c] = local[c * wrows : (c + 1) * wrows].astype(BF16)
    w1 = []
    for d in range(1, C):
        w1.append(send(w1_out.at[peer(d)], w1_in.at[d - 1], w1_s.at[d - 1], w1_r.at[d - 1], (row, peer(d))))
    sent += w1
    out_ref[0] = (pre * sigma).astype(BF16)
    put_out = fetch(out_ref, out_hbm, 8)

    for d in range(1, C):
        gb[d - 1].wait_recv()
    source = jnp.concatenate([gbuf[c] for c in range(C)], axis=1)

    part = w1_out[col].astype(F32)
    for d in range(1, C):
        w1[d - 1].wait_recv()
        part = part + w1_in[d - 1].astype(F32)
    w3[row] = part.astype(BF16)
    w3_sent = [
        send(w3.at[row], w3.at[row], w3_s.at[n], w3_r.at[n], ((row + n) % R, col)) for n in range(1, R)
    ]

    def back(i):
        cols = dense[:, pl.ds(pl.multiple_of(i * T, T), T)]
        return jnp.dot(source, cols, preferred_element_type=F32)

    yb = [None] * H
    far = list(range(2, H)) + [1]

    def back_y(k):
        yb_out[k] = back(z_of(k) * 2 + (1 - lo)).astype(BF16)
        yb[k] = send(yb_out.at[k], yb_in.at[k], yb_s.at[k], yb_r.at[k], (partner, col))

    for k in far + [0]:
        back_y(k)
    sent += yb

    zb = []

    def back_z(k):
        value = back(z_of(k) * 2 + lo)
        yb[k].wait_recv()
        zb_out[k] = (value + yb_in[k].astype(F32)).astype(BF16)
        zb.append(send(zb_out.at[k], zb_in.at[k], zb_s.at[k], zb_r.at[k], (z_of(k) * 2 + lo, col)))

    back_z(far[0])
    for copy in w3_sent:
        copy.wait_recv()
    whole = w3[0].astype(F32)
    for h in range(1, R):
        whole = whole + w3[h].astype(F32)
    w4[col] = (whole * scale).astype(BF16)
    w4_sent = [
        send(w4.at[col], w4.at[col], w4_s.at[d - 1], w4_r.at[d - 1], (row, peer(d))) for d in range(1, C)
    ]
    sent += w4_sent

    for k in far[1:]:
        back_z(k)
    sent += zb + w3_sent
    mine = back(hi * 2 + lo)
    yb[0].wait_recv()
    mine = mine + yb_in[0].astype(F32)

    for copy in zb:
        copy.wait_recv()
    for k in range(1, H):
        mine = mine + zb_in[k].astype(F32)
    gf_ref[0] = mine.T.astype(BF16)
    put_gf = fetch(gf_ref, gf_hbm, 9)

    for copy in w4_sent:
        copy.wait_recv()
    full = w4[...].astype(F32).reshape(2, wg_ref.shape[0], half)
    wg_ref[:, :half] = full[0]
    wg_ref[:, half:] = full[1]
    put_wg = fetch(wg_ref, wg_hbm, 10)
    for copy in sent:
        copy.wait_send()
    for copy in (put_out, put_gf, put_wg):
        copy.wait()


def hand_on(*refs):
    sources, targets, held, sem = refs[:3], refs[3:6], refs[6:9], refs[9]
    reads = [pltpu.make_async_copy(sources[n], held[n], sem.at[n]) for n in range(3)]
    writes = [pltpu.make_async_copy(held[n], targets[n], sem.at[3 + n]) for n in range(3)]
    for copy in reads:
        copy.start()
    for read, write in zip(reads, writes):
        read.wait()
        write.start()
    for copy in writes:
        copy.wait()


def on_device(features, weight, tile_values, tile_rows, tile_cols, tile_count, cotangent):
    T, width = features.shape[1], features.shape[2]
    hidden = weight.shape[1]
    R, C = lax.axis_size("row"), lax.axis_size("col")
    H = R // 2
    capacity = tile_values.shape[2]
    scale = (T * R * C) ** (-0.5)
    wrows = 2 * width // C
    width_links = -(-max(capacity, R * C) // 128) * 128
    hbm = pl.BlockSpec(memory_space=pltpu.HBM)

    def dma(n):
        return pltpu.SemaphoreType.DMA((n,))

    outs = (
        jax.ShapeDtypeStruct((1, T, hidden), BF16),
        jax.ShapeDtypeStruct((1, T, width), BF16),
        jax.ShapeDtypeStruct((width, hidden), F32),
    )
    results = pl.pallas_call(
        functools.partial(kernel, R, C, scale),
        out_shape=outs,
        in_specs=[hbm] * 7,
        out_specs=(hbm,) * 3,
        scratch_shapes=[
            pltpu.SMEM((1, 1, capacity), jnp.int32),
            pltpu.SMEM((1, 1, capacity), jnp.int32),
            pltpu.SMEM((1, 1), jnp.int32),
            pltpu.VMEM((2, width_links), jnp.int32),
            pltpu.SMEM((2, width_links), jnp.int32),
            pltpu.VMEM((width, hidden), BF16),
            *[pltpu.VMEM(o.shape, o.dtype) for o in outs],
            pltpu.VMEM((capacity, T, T), BF16),
            pltpu.VMEM((T, hidden), BF16),
            pltpu.VMEM((capacity + 1, T, T), F32),
            pltpu.VMEM((C * T, R * T), BF16),
            pltpu.VMEM((R, T, width), BF16),
            pltpu.VMEM((C - 1, T, width), BF16),
            pltpu.VMEM((C - 1, T, width), BF16),
            pltpu.VMEM((C, width, T), BF16),
            pltpu.VMEM((H, width, T), BF16),
            pltpu.VMEM((H, width, T), BF16),
            pltpu.VMEM((H, width, T), BF16),
            pltpu.VMEM((H, width, T), BF16),
            pltpu.VMEM((C, wrows, hidden // 2), BF16),
            pltpu.VMEM((C - 1, wrows, hidden // 2), BF16),
            pltpu.VMEM((R, wrows, hidden // 2), BF16),
            pltpu.VMEM((C, wrows, hidden // 2), BF16),
            dma(11),
            dma(H), dma(H), dma(H), dma(H), dma(C - 1), dma(C - 1), dma(C - 1), dma(C - 1),
            dma(H), dma(H), dma(H), dma(H), dma(C - 1), dma(C - 1),
            dma(R), dma(R), dma(C - 1), dma(C - 1),
        ],
        compiler_params=pltpu.CompilerParams(
            collective_id=0, has_side_effects=True, vmem_limit_bytes=60 * 1024 * 1024
        ),
    )(tile_rows, tile_cols, tile_count, features, weight, tile_values, cotangent)
    return pl.pallas_call(
        hand_on,
        out_shape=outs,
        in_specs=[hbm] * 3,
        out_specs=(hbm,) * 3,
        scratch_shapes=[*[pltpu.VMEM(o.shape, o.dtype) for o in outs], dma(6)],
        compiler_params=pltpu.CompilerParams(vmem_limit_bytes=60 * 1024 * 1024),
    )(*results)


def solution(mesh):
    placed = (
        P("col", "row", None),
        P(),
        P("row", "col", None, None, None),
        P("row", "col", None),
        P("row", "col", None),
        P("row", "col"),
        P("row", "col", None),
    )
    return jax.shard_map(
        on_device,
        mesh=mesh,
        in_specs=placed,
        out_specs=(P("row", "col", None), P("col", "row", None), P()),
        check_vma=False,
    )
```

```python
import functools

import jax
import jax.numpy as jnp
from jax import lax
from jax.experimental import pallas as pl
from jax.experimental.pallas import tpu as pltpu
from jax.sharding import PartitionSpec as P

MESH = pl.DeviceIdType.MESH
F32 = jnp.float32
BF16 = jnp.bfloat16


def fill_links(R, C, capacity, rows, cols, total, found):
    width = found.shape[1]
    lane = lax.broadcasted_iota(jnp.int32, (1, width), 1)
    count = total[0, 0]

    def key_of(t):
        return jnp.where(t < count, rows[0, 0, t] * R + cols[0, 0, t], -1)

    keys = jnp.full((1, width), -2, jnp.int32)
    for t in range(capacity):
        keys = jnp.where(lane == t, key_of(t), keys)
    before = jnp.full((1, width), capacity, jnp.int32)
    last = before
    for t in range(capacity):
        key = key_of(t)
        before = jnp.where((keys == key) & (lane > t), t, before)
        last = jnp.where(lane == key, t, last)
    found[0:1, :] = before
    found[1:2, :] = last


def kernel(
    R, C, scale,
    rows_ref, cols_ref, total_ref, feat_ref, weight_ref, tiles_ref, cot_ref,
    out_hbm, gf_hbm, wg_hbm,
    rows, cols, total_s, found, link_ref, w_ref, out_ref, gf_ref, wg_ref,
    tiles, cot, sums, dense, fbuf,
    agg_out, agg_in, gbuf, yb_out, yb_in, zb_out, zb_in,
    w1_out, w1_in, w3, w4,
    local_sem,
    za_s, za_r, ya_s, ya_r, ag_s, ag_r, gb_s, gb_r,
    yb_s, yb_r, zb_s, zb_r, w1_s, w1_r, w3_s, w3_r, w4_s, w4_r,
):
    row, col = lax.axis_index("row"), lax.axis_index("col")
    H = R // 2
    hi, lo = row // 2, row % 2
    partner = hi * 2 + (1 - lo)
    T = feat_ref.shape[1]
    capacity = tiles.shape[0]
    wrows = w4.shape[1]

    def peer(d):
        return (col + d) % C

    def z_of(k):
        other, bit = hi, 1
        while bit < H:
            if k & bit:
                other = other + bit * (1 - 2 * ((hi // bit) % 2))
            bit *= 2
        return other

    def send(src, dst, s, r, device):
        copy = pltpu.make_async_remote_copy(
            src_ref=src, dst_ref=dst, send_sem=s, recv_sem=r, device_id=device, device_id_type=MESH
        )
        copy.start()
        return copy

    def fetch(src, dst, n):
        copy = pltpu.make_async_copy(src, dst, local_sem.at[n])
        copy.start()
        return copy

    get_feat = fetch(feat_ref.at[0], fbuf.at[row], 0)
    get_ids = [fetch(rows_ref, rows, 1), fetch(cols_ref, cols, 2), fetch(total_ref, total_s, 3)]
    get_tiles = fetch(tiles_ref.at[0, 0], tiles, 4)
    get_w = fetch(weight_ref, w_ref, 5)
    get_cot = fetch(cot_ref.at[0], cot, 6)

    barrier = pltpu.get_barrier_semaphore()
    for n in range(1, R):
        pl.semaphore_signal(barrier, inc=1, device_id=((row + n) % R, col), device_id_type=MESH)
    for d in range(1, C):
        pl.semaphore_signal(barrier, inc=1, device_id=(row, peer(d)), device_id_type=MESH)
    get_feat.wait()
    pl.semaphore_wait(barrier, (R - 1) + (C - 1))

    sent = []
    own_y = send(fbuf.at[row], fbuf.at[row], ya_s.at[0], ya_r.at[0], (partner, col))
    za = [None]
    for k in range(1, H):
        za.append(send(fbuf.at[row], fbuf.at[row], za_s.at[k], za_r.at[k], (z_of(k) * 2 + lo, col)))

    near = send(fbuf.at[row], fbuf.at[row], ya_s.at[1], ya_r.at[1], (z_of(1) * 2 + 1 - lo, col))

    sums[capacity] = jnp.zeros(sums.shape[1:], F32)
    for copy in get_ids:
        copy.wait()
    fill_links(R, C, capacity, rows, cols, total_s, found)
    get_links = fetch(found, link_ref, 7)
    ya = [own_y, near]

    def forward(k):
        za[k].wait_recv()
        block = fbuf.at[z_of(k) * 2 + lo]
        ya.append(send(block, block, ya_s.at[k], ya_r.at[k], (partner, col)))

    get_tiles.wait()
    get_links.wait()

    def add_slot(t, carry):
        sums[t] = tiles[t].astype(F32) + sums[link_ref[0, t]]
        return carry

    lax.fori_loop(0, capacity, add_slot, 0, unroll=2)


    def place(b, carry):
        i, j = b // R, b % R
        dense[pl.ds(pl.multiple_of(i * T, T), T), pl.ds(pl.multiple_of(j * T, T), T)] = sums[
            link_ref[1, b]
        ].astype(BF16)
        return carry

    lax.fori_loop(0, R * C, place, 0, unroll=4)

    for k in range(2, H):
        forward(k)
    za[1].wait_recv()
    for k in range(H):
        ya[k].wait_recv()
    sent += za[1:] + ya

    def aggregate(j):
        rows = dense[pl.ds(pl.multiple_of(j * T, T), T), :]
        return jnp.dot(rows, fbuf[...].reshape(R * T, T), preferred_element_type=F32)

    ag = []
    for d in range(1, C):
        agg_out[d - 1] = aggregate(peer(d)).astype(BF16)
        ag.append(send(agg_out.at[d - 1], agg_in.at[d - 1], ag_s.at[d - 1], ag_r.at[d - 1], (row, peer(d))))
    total = aggregate(col)
    for d in range(1, C):
        ag[d - 1].wait_recv()
        total = total + agg_in[d - 1].astype(F32)
    sent += ag
    agg = total.astype(BF16)

    get_w.wait()
    get_cot.wait()
    pre = jnp.dot(agg, w_ref[...], preferred_element_type=F32)
    sigma = jax.nn.sigmoid(pre)
    slope = sigma * (1.0 + pre * (1.0 - sigma))
    grad_pre = (cot[...].astype(F32) * slope).astype(BF16)
    gbuf[col] = lax.dot_general(
        w_ref[...], grad_pre, (((1,), (1,)), ((), ())), preferred_element_type=F32
    ).astype(BF16)
    gb = []
    for d in range(1, C):
        gb.append(send(gbuf.at[col], gbuf.at[col], gb_s.at[d - 1], gb_r.at[d - 1], (row, peer(d))))
    sent += gb

    agg_t = agg.astype(F32).T.astype(BF16)
    local = jnp.dot(agg_t, grad_pre, preferred_element_type=F32)
    half = local.shape[1] // 2
    local = jnp.concatenate([local[:, :half], local[:, half:]], axis=0)
    for c in range(C):
        w1_out[c] = local[c * wrows : (c + 1) * wrows].astype(BF16)
    w1 = []
    for d in range(1, C):
        w1.append(send(w1_out.at[peer(d)], w1_in.at[d - 1], w1_s.at[d - 1], w1_r.at[d - 1], (row, peer(d))))
    sent += w1
    out_ref[0] = (pre * sigma).astype(BF16)
    put_out = fetch(out_ref, out_hbm, 8)

    for d in range(1, C):
        gb[d - 1].wait_recv()
    source = jnp.concatenate([gbuf[c] for c in range(C)], axis=1)

    part = w1_out[col].astype(F32)
    for d in range(1, C):
        w1[d - 1].wait_recv()
        part = part + w1_in[d - 1].astype(F32)
    w3[row] = part.astype(BF16)
    w3_sent = [
        send(w3.at[row], w3.at[row], w3_s.at[n], w3_r.at[n], ((row + n) % R, col)) for n in range(1, R)
    ]

    def back(i):
        cols = dense[:, pl.ds(pl.multiple_of(i * T, T), T)]
        return jnp.dot(source, cols, preferred_element_type=F32)

    yb = [None] * H
    far = list(range(2, H)) + [1]

    def back_y(k):
        yb_out[k] = back(z_of(k) * 2 + (1 - lo)).astype(BF16)
        yb[k] = send(yb_out.at[k], yb_in.at[k], yb_s.at[k], yb_r.at[k], (partner, col))

    for k in far + [0]:
        back_y(k)
    sent += yb

    zb = []

    def back_z(k):
        value = back(z_of(k) * 2 + lo)
        yb[k].wait_recv()
        zb_out[k] = (value + yb_in[k].astype(F32)).astype(BF16)
        zb.append(send(zb_out.at[k], zb_in.at[k], zb_s.at[k], zb_r.at[k], (z_of(k) * 2 + lo, col)))

    back_z(far[0])
    for copy in w3_sent:
        copy.wait_recv()
    whole = w3[0].astype(F32)
    for h in range(1, R):
        whole = whole + w3[h].astype(F32)
    w4[col] = (whole * scale).astype(BF16)
    w4_sent = [
        send(w4.at[col], w4.at[col], w4_s.at[d - 1], w4_r.at[d - 1], (row, peer(d))) for d in range(1, C)
    ]
    sent += w4_sent

    for k in far[1:]:
        back_z(k)
    sent += zb + w3_sent
    mine = back(hi * 2 + lo)
    yb[0].wait_recv()
    mine = mine + yb_in[0].astype(F32)

    for copy in zb:
        copy.wait_recv()
    for k in range(1, H):
        mine = mine + zb_in[k].astype(F32)
    gf_ref[0] = mine.T.astype(BF16)
    put_gf = fetch(gf_ref, gf_hbm, 9)

    for copy in w4_sent:
        copy.wait_recv()
    full = w4[...].astype(F32).reshape(2, wg_ref.shape[0], half)
    wg_ref[:, :half] = full[0]
    wg_ref[:, half:] = full[1]
    put_wg = fetch(wg_ref, wg_hbm, 10)
    for copy in sent:
        copy.wait_send()
    for copy in (put_out, put_gf, put_wg):
        copy.wait()


def hand_on(*refs):
    sources, targets, held, sem = refs[:3], refs[3:6], refs[6:9], refs[9]
    reads = [pltpu.make_async_copy(sources[n], held[n], sem.at[n]) for n in range(3)]
    writes = [pltpu.make_async_copy(held[n], targets[n], sem.at[3 + n]) for n in range(3)]
    for copy in reads:
        copy.start()
    for read, write in zip(reads, writes):
        read.wait()
        write.start()
    for copy in writes:
        copy.wait()


def on_device(features, weight, tile_values, tile_rows, tile_cols, tile_count, cotangent):
    T, width = features.shape[1], features.shape[2]
    hidden = weight.shape[1]
    R, C = lax.axis_size("row"), lax.axis_size("col")
    H = R // 2
    capacity = tile_values.shape[2]
    scale = (T * R * C) ** (-0.5)
    wrows = 2 * width // C
    width_links = -(-max(capacity, R * C) // 128) * 128
    hbm = pl.BlockSpec(memory_space=pltpu.HBM)

    def dma(n):
        return pltpu.SemaphoreType.DMA((n,))

    outs = (
        jax.ShapeDtypeStruct((1, T, hidden), BF16),
        jax.ShapeDtypeStruct((1, T, width), BF16),
        jax.ShapeDtypeStruct((width, hidden), F32),
    )
    results = pl.pallas_call(
        functools.partial(kernel, R, C, scale),
        out_shape=outs,
        in_specs=[hbm] * 7,
        out_specs=(hbm,) * 3,
        scratch_shapes=[
            pltpu.SMEM((1, 1, capacity), jnp.int32),
            pltpu.SMEM((1, 1, capacity), jnp.int32),
            pltpu.SMEM((1, 1), jnp.int32),
            pltpu.VMEM((2, width_links), jnp.int32),
            pltpu.SMEM((2, width_links), jnp.int32),
            pltpu.VMEM((width, hidden), BF16),
            *[pltpu.VMEM(o.shape, o.dtype) for o in outs],
            pltpu.VMEM((capacity, T, T), BF16),
            pltpu.VMEM((T, hidden), BF16),
            pltpu.VMEM((capacity + 1, T, T), F32),
            pltpu.VMEM((C * T, R * T), BF16),
            pltpu.VMEM((R, T, width), BF16),
            pltpu.VMEM((C - 1, T, width), BF16),
            pltpu.VMEM((C - 1, T, width), BF16),
            pltpu.VMEM((C, width, T), BF16),
            pltpu.VMEM((H, width, T), BF16),
            pltpu.VMEM((H, width, T), BF16),
            pltpu.VMEM((H, width, T), BF16),
            pltpu.VMEM((H, width, T), BF16),
            pltpu.VMEM((C, wrows, hidden // 2), BF16),
            pltpu.VMEM((C - 1, wrows, hidden // 2), BF16),
            pltpu.VMEM((R, wrows, hidden // 2), BF16),
            pltpu.VMEM((C, wrows, hidden // 2), BF16),
            dma(11),
            dma(H), dma(H), dma(H), dma(H), dma(C - 1), dma(C - 1), dma(C - 1), dma(C - 1),
            dma(H), dma(H), dma(H), dma(H), dma(C - 1), dma(C - 1),
            dma(R), dma(R), dma(C - 1), dma(C - 1),
        ],
        compiler_params=pltpu.CompilerParams(
            collective_id=0, has_side_effects=True, vmem_limit_bytes=60 * 1024 * 1024
        ),
    )(tile_rows, tile_cols, tile_count, features, weight, tile_values, cotangent)
    return pl.pallas_call(
        hand_on,
        out_shape=outs,
        in_specs=[hbm] * 3,
        out_specs=(hbm,) * 3,
        scratch_shapes=[*[pltpu.VMEM(o.shape, o.dtype) for o in outs], dma(6)],
        compiler_params=pltpu.CompilerParams(vmem_limit_bytes=60 * 1024 * 1024),
    )(*results)


def solution(mesh):
    placed = (
        P("col", "row", None),
        P(),
        P("row", "col", None, None, None),
        P("row", "col", None),
        P("row", "col", None),
        P("row", "col"),
        P("row", "col", None),
    )
    return jax.shard_map(
        on_device,
        mesh=mesh,
        in_specs=placed,
        out_specs=(P("row", "col", None), P("col", "row", None), P()),
        check_vma=False,
    )
```
